32 devices in a mesh: row: 4 (over z), col: 4 (over y, x), filt: 2 (over core).
Axes of the slice: x: 2, y: 2, z: 4, core: 2. Of those that a mesh axis runs over, the one named last changes fastest.
Arguments:
- grad_out: bfloat16 [16, 128, 64, 256], P(None, 'row', 'col', 'filt'), may hold values from -6 to 6
- pre_act: bfloat16 [16, 128, 64, 256], P(None, 'row', 'col', 'filt'), may hold values from -6 to 6
- weight_one: bfloat16 [3, 3, 256, 256], replicated, may hold values from -0.125 to 0.125
- weight_two: bfloat16 [3, 3, 256, 256], replicated, may hold values from -0.125 to 0.125
Outputs:
- grad_in: bfloat16 [16, 128, 64, 256], P(None, 'row', 'col', 'filt')
The draws below stay inside these ranges and needn't reach their ends.
All inputs are finite; a program needn't handle non-finite values.
Results may differ from the reference program's by a relative error of at most 0.0049.
Values may be sent and summed in bfloat16 or wider, within the bound.
A program may use at most 192 MiB of HBM per device.

```python
import jax
import jax.numpy as jnp

C = 256
BATCH = 16
H = 128
W = 64


def block_scale(rng, extent, cuts, low, largest):
    def one(position, blocks):
        draws = jax.random.uniform(jax.random.fold_in(jax.random.fold_in(rng, 6), position), (blocks,), jnp.float32, low / len(cuts), largest / len(cuts))
        return jnp.repeat(jnp.exp(draws), extent[position] // blocks).reshape((-1,) + (1,) * (len(extent) - position - 1))

    level = one(*cuts[0])
    for cut in cuts[1:]:
        level = level * one(*cut)
    return level


def noise(key, shape, width, bound, split=(), kind=jnp.bfloat16):
    drawn = jax.random.normal(key, shape, jnp.float32) * width
    if len(split) > 0:
        drawn = block_scale(key, shape, split, -0.22, 0.18) * drawn
    return jnp.clip(drawn, min=-bound, max=bound).astype(kind)


def setup_inputs(seed: int = 0) -> dict:
    keys = jax.random.split(jax.random.key(seed), 5)
    grad_out = noise(keys[0], (BATCH, H, W, C), 1.0, 6.0, ((1, 4), (2, 4), (3, 2)))
    pre_act = noise(keys[1], (BATCH, H, W, C), 1.0, 6.0, ((1, 4), (2, 4), (3, 2)))
    weight_one = noise(keys[2], (3, 3, C, C), (9 * C) ** -0.5, 0.125)
    weight_two = noise(keys[3], (3, 3, C, C), (9 * C) ** -0.5, 0.125)
    return dict(grad_out=grad_out, pre_act=pre_act, weight_one=weight_one, weight_two=weight_two)


def back_conv(grad, weight, spacing):
    rows = grad.shape[1]
    cols = grad.shape[2]
    padded = jnp.pad(grad.astype(jnp.float32), ((0, 0), (spacing, spacing), (spacing, spacing), (0, 0)))
    total = jnp.zeros(grad.shape[:3] + (weight.shape[2],), jnp.float32)
    for tap_row in range(3):
        for tap_col in range(3):
            top = spacing * (2 - tap_row)
            left = spacing * (2 - tap_col)
            piece = padded[:, top:top + rows, left:left + cols, :]
            total = total + jnp.einsum("bhwo,io->bhwi", piece, weight[tap_row, tap_col].astype(jnp.float32))
    return total


def reference(grad_out, pre_act, weight_one, weight_two):
    grad_a = back_conv(grad_out, weight_two, 4)
    grad_h = jnp.where(pre_act > 0, grad_a, jnp.float32(0.0)).astype(jnp.bfloat16)
    return back_conv(grad_h, weight_one, 2).astype(jnp.bfloat16)
```

```python
import functools

import jax
import jax.numpy as jnp
from jax import lax
from jax.experimental import pallas as pl
from jax.experimental.pallas import tpu as pltpu
from jax.sharding import PartitionSpec as P

MESH = pl.DeviceIdType.MESH
GS = 4
HS = 2


def conv(buf, weight, row, col, rows, cols, spacing):
    batch = buf.shape[3]
    pieces = []
    for p in range(3):
        for q in range(3):
            for half in range(2):
                piece = buf[half, pl.ds(row + spacing * (2 - p), rows), pl.ds(col + spacing * (2 - q), cols)]
                pieces.append(piece.reshape(rows * cols * batch, piece.shape[-1]))
    return jnp.dot(jnp.concatenate(pieces, axis=1), weight[...], preferred_element_type=jnp.float32)


def kernel(nrow, ncol, g_in, p_in, w1, w2, out, gbuf, pbuf, hbuf, obuf, send, recv, local):
    r, c, f = lax.axis_index("row"), lax.axis_index("col"), lax.axis_index("filt")
    o = 1 - f
    rows = g_in.shape[0] // 2
    cols = g_in.shape[1]
    batch, chan = g_in.shape[2], g_in.shape[3]
    has_left, has_right = c > 0, c < ncol - 1
    has_top, has_bot = r > 0, r < nrow - 1
    first, last = jnp.logical_and(f == 0, r == 0), jnp.logical_and(f == 1, r == nrow - 1)
    has_up, has_down = jnp.logical_not(first), jnp.logical_not(last)
    up = (r - o, c, o)
    down = (r + f, c, o)
    partner = (r, c, o)

    @pl.when(first)
    def _():
        gbuf[:, :GS] = jnp.zeros((2, GS) + gbuf.shape[2:], gbuf.dtype)
        hbuf[:, :HS] = jnp.zeros((2, HS) + hbuf.shape[2:], hbuf.dtype)

    @pl.when(last)
    def _():
        gbuf[:, rows + GS:] = jnp.zeros((2, GS) + gbuf.shape[2:], gbuf.dtype)
        hbuf[:, rows + HS:] = jnp.zeros((2, HS) + hbuf.shape[2:], hbuf.dtype)

    @pl.when(jnp.logical_not(has_left))
    def _():
        gbuf[:, :, :GS] = jnp.zeros((2, rows + 2 * GS, GS, batch, chan), gbuf.dtype)
        hbuf[:, :, :HS] = jnp.zeros((2, rows + 2 * HS, HS, batch, chan), hbuf.dtype)

    @pl.when(jnp.logical_not(has_right))
    def _():
        gbuf[:, :, cols + GS:] = jnp.zeros((2, rows + 2 * GS, GS, batch, chan), gbuf.dtype)
        hbuf[:, :, cols + HS:] = jnp.zeros((2, rows + 2 * HS, HS, batch, chan), hbuf.dtype)

    barrier = pltpu.get_barrier_semaphore()
    pl.semaphore_signal(barrier, inc=1, device_id=partner, device_id_type=MESH)
    count = jnp.int32(1)
    for there, rr, cc in ((has_left, r, c - 1), (has_right, r, c + 1), (has_top, r - 1, c), (has_bot, r + 1, c)):
        @pl.when(there)
        def _(rr=rr, cc=cc):
            for ff in range(2):
                pl.semaphore_signal(barrier, inc=1, device_id=(rr, cc, ff), device_id_type=MESH)
        count = count + jnp.where(there, 2, 0)
    pl.semaphore_wait(barrier, count)

    def copy(src, dst, sidx, ridx, device):
        return pltpu.make_async_remote_copy(
            src_ref=src, dst_ref=dst, send_sem=send.at[sidx], recv_sem=recv.at[ridx],
            device_id=device, device_id_type=MESH)

    def landed(dst, ridx):
        copy(dst, dst, 0, ridx, partner).wait_recv()

    sends = []

    def start(there, src, dst, ridx, device):
        sidx = len(sends)
        what = copy(src, dst, sidx, ridx, device)
        sends.append((there, what))
        if there is None:
            what.start()
        else:
            @pl.when(there)
            def _():
                what.start()

    grow, gcol = pl.ds(GS, rows), pl.ds(GS, cols)
    hrow, hcol = pl.ds(HS, rows), pl.ds(HS, cols)
    L, R, T, B, MAIN, PRE, CORNER, HL, HR, HT, HB, HCORNER, OUT = 0, 2, 4, 6, 8, 9, 10, 14, 15, 16, 17, 18, 22

    for ff in range(2):
        start(has_right, g_in.at[pl.ds(rows * ff, rows), pl.ds(cols - GS, GS)], gbuf.at[f, grow, pl.ds(0, GS)],
              L + f, (r, c + 1, ff))
        start(has_left, g_in.at[pl.ds(rows * ff, rows), pl.ds(0, GS)], gbuf.at[f, grow, pl.ds(cols + GS, GS)],
              R + f, (r, c - 1, ff))
    span = rows + GS
    start(None, g_in.at[pl.ds((rows - GS) * o, span)], gbuf.at[f, pl.ds(GS * f, span), gcol], MAIN, partner)
    mine = pltpu.make_async_copy(
        g_in.at[pl.ds((rows - GS) * f, span)], gbuf.at[f, pl.ds(GS * o, span), gcol], local.at[0])
    mine.start()
    start(has_bot, g_in.at[pl.ds(2 * rows - GS, GS)], gbuf.at[f, pl.ds(0, GS), gcol], T + f, (r + 1, c, 0))
    start(has_top, g_in.at[pl.ds(0, GS)], gbuf.at[f, pl.ds(rows + GS, GS), gcol], B + f, (r - 1, c, 1))
    start(None, p_in.at[pl.ds(rows * o, rows)], pbuf.at[f], PRE, partner)
    own_pre = pltpu.make_async_copy(p_in.at[pl.ds(rows * f, rows)], pbuf.at[f], local.at[1])
    own_pre.start()

    landed(gbuf.at[o, pl.ds(GS * o, span), gcol], MAIN)
    mine.wait()
    landed(pbuf.at[o], PRE)
    own_pre.wait()

    @pl.when(jnp.logical_and(f == 0, has_top))
    def _():
        for half in range(2):
            landed(gbuf.at[half, pl.ds(0, GS), gcol], T + half)

    @pl.when(jnp.logical_and(f == 1, has_bot))
    def _():
        for half in range(2):
            landed(gbuf.at[half, pl.ds(rows + GS, GS), gcol], B + half)

    def hidden(row, col, nr, nc):
        total = conv(gbuf, w2, row, col, nr, nc, GS)
        for half in range(2):
            keep = pbuf[half, pl.ds(row, nr), pl.ds(col, nc)].reshape(nr * nc * batch, chan).astype(jnp.float32) > 0
            part = jnp.where(keep, total[:, half * chan:(half + 1) * chan], 0.0).astype(hbuf.dtype)
            hbuf[half, pl.ds(row + HS, nr), pl.ds(col + HS, nc)] = part.reshape(nr, nc, batch, chan)

    @pl.loop(0, rows // 4)
    def _(i):
        hidden(i * 4, GS, 4, cols - 2 * GS)

    @pl.when(has_left)
    def _():
        for half in range(2):
            landed(gbuf.at[half, grow, pl.ds(0, GS)], L + half)

    @pl.when(has_right)
    def _():
        for half in range(2):
            landed(gbuf.at[half, grow, pl.ds(cols + GS, GS)], R + half)

    both = pl.ds(0, 2)

    def corners(buf, width, size, base):
        for side, there, col in ((0, has_left, 0), (1, has_right, cols + width)):
            at = pl.ds(col, width)
            start(jnp.logical_and(there, has_up), buf.at[both, pl.ds(width, width), at],
                  buf.at[both, pl.ds(rows + width, width), at], base + side, up)
            start(jnp.logical_and(there, has_down), buf.at[both, pl.ds(rows, width), at],
                  buf.at[both, pl.ds(0, width), at], base + 2 + side, down)

    def corners_landed(buf, width, base):
        for side, there, col in ((0, has_left, 0), (1, has_right, cols + width)):
            at = pl.ds(col, width)

            @pl.when(jnp.logical_and(there, has_down))
            def _(side=side, at=at):
                landed(buf.at[both, pl.ds(rows + width, width), at], base + side)

            @pl.when(jnp.logical_and(there, has_up))
            def _(side=side, at=at):
                landed(buf.at[both, pl.ds(0, width), at], base + 2 + side)

    corners(gbuf, GS, GS, CORNER)

    @pl.loop(1, rows // 4 - 1)
    def _(i):
        hidden(i * 4, 0, 4, GS)
        hidden(i * 4, cols - GS, 4, GS)

    corners_landed(gbuf, GS, CORNER)

    @pl.loop(0, 2)
    def _(i):
        at = i * (rows - 4)
        hidden(at, 0, 4, GS)
        hidden(at, cols - GS, 4, GS)

    start(has_right, hbuf.at[both, hrow, pl.ds(cols, HS)], hbuf.at[both, hrow, pl.ds(0, HS)], HL, (r, c + 1, f))
    start(has_left, hbuf.at[both, hrow, pl.ds(HS, HS)], hbuf.at[both, hrow, pl.ds(cols + HS, HS)], HR, (r, c - 1, f))
    start(has_up, hbuf.at[both, pl.ds(HS, HS), hcol], hbuf.at[both, pl.ds(rows + HS, HS), hcol], HB, up)
    start(has_down, hbuf.at[both, pl.ds(rows, HS), hcol], hbuf.at[both, pl.ds(0, HS), hcol], HT, down)

    def result(row, col, nr, nc):
        total = conv(hbuf, w1, row, col, nr, nc, HS)
        for half in range(2):
            part = total[:, half * chan:(half + 1) * chan].astype(obuf.dtype)
            obuf[half, pl.ds(row, nr), pl.ds(col, nc)] = part.reshape(nr, nc, batch, chan)

    @pl.loop(0, (rows - 2 * HS) // 4)
    def _(i):
        result(HS + i * 4, HS, 4, cols - 2 * HS)

    @pl.when(has_up)
    def _():
        landed(hbuf.at[both, pl.ds(0, HS), hcol], HT)

    @pl.when(has_down)
    def _():
        landed(hbuf.at[both, pl.ds(rows + HS, HS), hcol], HB)

    @pl.loop(0, 2)
    def _(i):
        result(i * (rows - HS), HS, HS, cols - 2 * HS)

    @pl.when(has_left)
    def _():
        landed(hbuf.at[both, hrow, pl.ds(0, HS)], HL)

    @pl.when(has_right)
    def _():
        landed(hbuf.at[both, hrow, pl.ds(cols + HS, HS)], HR)

    corners(hbuf, HS, HS, HCORNER)

    @pl.loop(0, 2)
    def _(i):
        result(HS, i * (cols - HS), rows - 2 * HS, HS)

    corners_landed(hbuf, HS, HCORNER)

    @pl.loop(0, 2)
    def _(i):
        result(i * (rows - HS), 0, HS, HS)
        result(i * (rows - HS), cols - HS, HS, HS)

    start(None, obuf.at[o], out.at[pl.ds(rows * f, rows)], OUT, partner)
    keep = pltpu.make_async_copy(obuf.at[f], out.at[pl.ds(rows * f, rows)], local.at[2])
    keep.start()
    landed(out.at[pl.ds(rows * o, rows)], OUT)
    keep.wait()
    for there, what in sends:
        if there is None:
            what.wait_send()
        else:
            @pl.when(there)
            def _(what=what):
                what.wait_send()


def solution(mesh):
    nrow, ncol = mesh.shape["row"], mesh.shape["col"]

    def per_device(grad_out, pre_act, weight_one, weight_two):
        batch, rows, cols, chan = grad_out.shape
        taps = lambda w: jnp.swapaxes(w, 2, 3).reshape(-1, w.shape[2])
        inward = lambda a: jnp.transpose(a, (1, 2, 0, 3))
        strip = rows // 2
        kind = grad_out.dtype
        out = pl.pallas_call(
            functools.partial(kernel, nrow, ncol),
            out_shape=jax.ShapeDtypeStruct((rows, cols, batch, chan), kind),
            in_specs=[pl.BlockSpec(memory_space=pl.ANY)] * 2 + [pl.BlockSpec(memory_space=pltpu.VMEM)] * 2,
            out_specs=pl.BlockSpec(memory_space=pl.ANY),
            scratch_shapes=[
                pltpu.VMEM((2, strip + 2 * GS, cols + 2 * GS, batch, chan), kind),
                pltpu.VMEM((2, strip, cols, batch, chan), kind),
                pltpu.VMEM((2, strip + 2 * HS, cols + 2 * HS, batch, chan), kind),
                pltpu.VMEM((2, strip, cols, batch, chan), kind),
                pltpu.SemaphoreType.DMA((24,)),
                pltpu.SemaphoreType.DMA((23,)),
                pltpu.SemaphoreType.DMA((3,)),
            ],
            compiler_params=pltpu.CompilerParams(
                collective_id=0, has_side_effects=True, vmem_limit_bytes=48 * 1024 * 1024),
            cost_estimate=pl.CostEstimate(
                flops=4 * 9 * batch * rows * cols * chan * 2 * chan, bytes_accessed=8 * batch * rows * cols * chan,
                transcendentals=0),
        )(inward(grad_out), inward(pre_act), taps(weight_one), taps(weight_two))
        return jnp.transpose(out, (2, 0, 1, 3))

    placed = (P(None, "row", "col", "filt"), P(None, "row", "col", "filt"), P(), P())
    return jax.shard_map(
        per_device, mesh=mesh, in_specs=placed, out_specs=P(None, "row", "col", "filt"), check_vma=False)
```

```python
import functools

import jax
import jax.numpy as jnp
from jax import lax
from jax.experimental import pallas as pl
from jax.experimental.pallas import tpu as pltpu
from jax.sharding import PartitionSpec as P

MESH = pl.DeviceIdType.MESH
GS = 4
HS = 2


def conv(buf, weight, row, col, rows, cols, spacing):
    batch = buf.shape[3]
    pieces = []
    for p in range(3):
        for q in range(3):
            for half in range(2):
                piece = buf[half, pl.ds(row + spacing * (2 - p), rows), pl.ds(col + spacing * (2 - q), cols)]
                pieces.append(piece.reshape(rows * cols * batch, piece.shape[-1]))
    return jnp.dot(jnp.concatenate(pieces, axis=1), weight[...], preferred_element_type=jnp.float32)


def kernel(nrow, ncol, g_in, p_in, w1, w2, out, gbuf, pbuf, hbuf, obuf, gvia, hvia, send, recv, local):
    r, c, f = lax.axis_index("row"), lax.axis_index("col"), lax.axis_index("filt")
    o = 1 - f
    rows = g_in.shape[0] // 2
    cols = g_in.shape[1]
    batch, chan = g_in.shape[2], g_in.shape[3]
    has_left, has_right = c > 0, c < ncol - 1
    has_top, has_bot = r > 0, r < nrow - 1
    first, last = jnp.logical_and(f == 0, r == 0), jnp.logical_and(f == 1, r == nrow - 1)
    has_up, has_down = jnp.logical_not(first), jnp.logical_not(last)
    up = (r - o, c, o)
    down = (r + f, c, o)
    partner = (r, c, o)
    folded = ncol == 4
    across = lax.rem(c + 2, 4)

    @pl.when(first)
    def _():
        gbuf[:, :GS] = jnp.zeros((2, GS) + gbuf.shape[2:], gbuf.dtype)
        hbuf[:, :HS] = jnp.zeros((2, HS) + hbuf.shape[2:], hbuf.dtype)

    @pl.when(last)
    def _():
        gbuf[:, rows + GS:] = jnp.zeros((2, GS) + gbuf.shape[2:], gbuf.dtype)
        hbuf[:, rows + HS:] = jnp.zeros((2, HS) + hbuf.shape[2:], hbuf.dtype)

    @pl.when(jnp.logical_not(has_left))
    def _():
        gbuf[:, :, :GS] = jnp.zeros((2, rows + 2 * GS, GS, batch, chan), gbuf.dtype)
        hbuf[:, :, :HS] = jnp.zeros((2, rows + 2 * HS, HS, batch, chan), hbuf.dtype)

    @pl.when(jnp.logical_not(has_right))
    def _():
        gbuf[:, :, cols + GS:] = jnp.zeros((2, rows + 2 * GS, GS, batch, chan), gbuf.dtype)
        hbuf[:, :, cols + HS:] = jnp.zeros((2, rows + 2 * HS, HS, batch, chan), hbuf.dtype)

    barrier = pltpu.get_barrier_semaphore()
    pl.semaphore_signal(barrier, inc=1, device_id=partner, device_id_type=MESH)
    count = jnp.int32(1)
    for there, rr, cc in ((has_left, r, c - 1), (has_right, r, c + 1), (has_top, r - 1, c), (has_bot, r + 1, c)):
        @pl.when(there)
        def _(rr=rr, cc=cc):
            for ff in range(2):
                pl.semaphore_signal(barrier, inc=1, device_id=(rr, cc, ff), device_id_type=MESH)
        count = count + jnp.where(there, 2, 0)
    if folded:
        pl.semaphore_signal(barrier, inc=1, device_id=(r, across, f), device_id_type=MESH)
        count = count + 1
    pl.semaphore_wait(barrier, count)

    def copy(src, dst, sidx, ridx, device):
        return pltpu.make_async_remote_copy(
            src_ref=src, dst_ref=dst, send_sem=send.at[sidx], recv_sem=recv.at[ridx],
            device_id=device, device_id_type=MESH)

    def landed(dst, ridx):
        copy(dst, dst, 0, ridx, partner).wait_recv()

    sends = []

    def start(there, src, dst, ridx, device):
        sidx = len(sends)
        what = copy(src, dst, sidx, ridx, device)
        sends.append((there, what))
        if there is None:
            what.start()
        else:
            @pl.when(there)
            def _():
                what.start()

    grow, gcol = pl.ds(GS, rows), pl.ds(GS, cols)
    hrow, hcol = pl.ds(HS, rows), pl.ds(HS, cols)
    L, R, T, B, MAIN, PRE, CORNER, HL, HR, HT, HB, HCORNER, OUT, VIA, HVIA = (
        0, 2, 4, 6, 8, 9, 10, 14, 15, 16, 17, 18, 22, 23, 24)

    if folded:
        start(c == 1, g_in.at[pl.ds(rows, rows), pl.ds(cols - GS, GS)], gvia, VIA, (r, across, f))
        start(c == 2, g_in.at[pl.ds(rows, rows), pl.ds(0, GS)], gvia, VIA, (r, across, f))
    for ff in range(2):
        to_right, to_left = has_right, has_left
        if folded and ff == 1:
            to_right = jnp.logical_and(has_right, c != 1)
            to_left = jnp.logical_and(has_left, c != 2)
        start(to_right, g_in.at[pl.ds(rows * ff, rows), pl.ds(cols - GS, GS)], gbuf.at[f, grow, pl.ds(0, GS)],
              L + f, (r, c + 1, ff))
        start(to_left, g_in.at[pl.ds(rows * ff, rows), pl.ds(0, GS)], gbuf.at[f, grow, pl.ds(cols + GS, GS)],
              R + f, (r, c - 1, ff))
    span = rows + GS
    start(None, g_in.at[pl.ds((rows - GS) * o, span)], gbuf.at[f, pl.ds(GS * f, span), gcol], MAIN, partner)
    mine = pltpu.make_async_copy(
        g_in.at[pl.ds((rows - GS) * f, span)], gbuf.at[f, pl.ds(GS * o, span), gcol], local.at[0])
    mine.start()
    start(has_bot, g_in.at[pl.ds(2 * rows - GS, GS)], gbuf.at[f, pl.ds(0, GS), gcol], T + f, (r + 1, c, 0))
    start(has_top, g_in.at[pl.ds(0, GS)], gbuf.at[f, pl.ds(rows + GS, GS), gcol], B + f, (r - 1, c, 1))
    start(None, p_in.at[pl.ds(rows * o, rows)], pbuf.at[f], PRE, partner)
    own_pre = pltpu.make_async_copy(p_in.at[pl.ds(rows * f, rows)], pbuf.at[f], local.at[1])
    own_pre.start()

    if folded:
        @pl.when(jnp.logical_or(c == 0, c == 3))
        def _():
            landed(gvia, VIA)
        start(c == 3, gvia, gbuf.at[f, grow, pl.ds(0, GS)], L + f, (r, c - 1, 1))
        start(c == 0, gvia, gbuf.at[f, grow, pl.ds(cols + GS, GS)], R + f, (r, c + 1, 1))

    landed(gbuf.at[o, pl.ds(GS * o, span), gcol], MAIN)
    mine.wait()
    landed(pbuf.at[o], PRE)
    own_pre.wait()

    @pl.when(jnp.logical_and(f == 0, has_top))
    def _():
        for half in range(2):
            landed(gbuf.at[half, pl.ds(0, GS), gcol], T + half)

    @pl.when(jnp.logical_and(f == 1, has_bot))
    def _():
        for half in range(2):
            landed(gbuf.at[half, pl.ds(rows + GS, GS), gcol], B + half)

    def hidden(row, col, nr, nc):
        total = conv(gbuf, w2, row, col, nr, nc, GS)
        for half in range(2):
            keep = pbuf[half, pl.ds(row, nr), pl.ds(col, nc)].reshape(nr * nc * batch, chan).astype(jnp.float32) > 0
            part = jnp.where(keep, total[:, half * chan:(half + 1) * chan], 0.0).astype(hbuf.dtype)
            hbuf[half, pl.ds(row + HS, nr), pl.ds(col + HS, nc)] = part.reshape(nr, nc, batch, chan)

    @pl.loop(0, rows // 4)
    def _(i):
        hidden(i * 4, GS, 4, cols - 2 * GS)

    @pl.when(has_left)
    def _():
        for half in range(2):
            landed(gbuf.at[half, grow, pl.ds(0, GS)], L + half)

    @pl.when(has_right)
    def _():
        for half in range(2):
            landed(gbuf.at[half, grow, pl.ds(cols + GS, GS)], R + half)

    both = pl.ds(0, 2)

    def corners(buf, width, size, base):
        for side, there, col in ((0, has_left, 0), (1, has_right, cols + width)):
            at = pl.ds(col, width)
            start(jnp.logical_and(there, has_up), buf.at[both, pl.ds(width, width), at],
                  buf.at[both, pl.ds(rows + width, width), at], base + side, up)
            start(jnp.logical_and(there, has_down), buf.at[both, pl.ds(rows, width), at],
                  buf.at[both, pl.ds(0, width), at], base + 2 + side, down)

    def corners_landed(buf, width, base):
        for side, there, col in ((0, has_left, 0), (1, has_right, cols + width)):
            at = pl.ds(col, width)

            @pl.when(jnp.logical_and(there, has_down))
            def _(side=side, at=at):
                landed(buf.at[both, pl.ds(rows + width, width), at], base + side)

            @pl.when(jnp.logical_and(there, has_up))
            def _(side=side, at=at):
                landed(buf.at[both, pl.ds(0, width), at], base + 2 + side)

    corners(gbuf, GS, GS, CORNER)

    @pl.loop(1, rows // 4 - 1)
    def _(i):
        hidden(i * 4, 0, 4, GS)
        hidden(i * 4, cols - GS, 4, GS)

    corners_landed(gbuf, GS, CORNER)

    @pl.loop(0, 2)
    def _(i):
        at = i * (rows - 4)
        hidden(at, 0, 4, GS)
        hidden(at, cols - GS, 4, GS)

    to_right, to_left = has_right, has_left
    if folded:
        start(jnp.logical_and(c == 1, f == 1), hbuf.at[both, hrow, pl.ds(cols, HS)], hvia, HVIA, (r, across, f))
        start(jnp.logical_and(c == 2, f == 1), hbuf.at[both, hrow, pl.ds(HS, HS)], hvia, HVIA, (r, across, f))
        to_right = jnp.logical_and(has_right, jnp.logical_or(c != 1, f == 0))
        to_left = jnp.logical_and(has_left, jnp.logical_or(c != 2, f == 0))
    start(to_right, hbuf.at[both, hrow, pl.ds(cols, HS)], hbuf.at[both, hrow, pl.ds(0, HS)], HL, (r, c + 1, f))
    start(to_left, hbuf.at[both, hrow, pl.ds(HS, HS)], hbuf.at[both, hrow, pl.ds(cols + HS, HS)], HR, (r, c - 1, f))
    start(has_up, hbuf.at[both, pl.ds(HS, HS), hcol], hbuf.at[both, pl.ds(rows + HS, HS), hcol], HB, up)
    start(has_down, hbuf.at[both, pl.ds(rows, HS), hcol], hbuf.at[both, pl.ds(0, HS), hcol], HT, down)

    def result(row, col, nr, nc):
        total = conv(hbuf, w1, row, col, nr, nc, HS)
        for half in range(2):
            part = total[:, half * chan:(half + 1) * chan].astype(obuf.dtype)
            obuf[half, pl.ds(row, nr), pl.ds(col, nc)] = part.reshape(nr, nc, batch, chan)

    @pl.loop(0, (rows - 2 * HS) // 4)
    def _(i):
        result(HS + i * 4, HS, 4, cols - 2 * HS)

    if folded:
        @pl.when(jnp.logical_and(jnp.logical_or(c == 0, c == 3), f == 1))
        def _():
            landed(hvia, HVIA)
        start(jnp.logical_and(c == 3, f == 1), hvia, hbuf.at[both, hrow, pl.ds(0, HS)], HL, (r, c - 1, f))
        start(jnp.logical_and(c == 0, f == 1), hvia, hbuf.at[both, hrow, pl.ds(cols + HS, HS)], HR, (r, c + 1, f))

    @pl.when(has_up)
    def _():
        landed(hbuf.at[both, pl.ds(0, HS), hcol], HT)

    @pl.when(has_down)
    def _():
        landed(hbuf.at[both, pl.ds(rows + HS, HS), hcol], HB)

    @pl.loop(0, 2)
    def _(i):
        result(i * (rows - HS), HS, HS, cols - 2 * HS)

    @pl.when(has_left)
    def _():
        landed(hbuf.at[both, hrow, pl.ds(0, HS)], HL)

    @pl.when(has_right)
    def _():
        landed(hbuf.at[both, hrow, pl.ds(cols + HS, HS)], HR)

    corners(hbuf, HS, HS, HCORNER)

    @pl.loop(0, 2)
    def _(i):
        result(HS, i * (cols - HS), rows - 2 * HS, HS)

    corners_landed(hbuf, HS, HCORNER)

    @pl.loop(0, 2)
    def _(i):
        result(i * (rows - HS), 0, HS, HS)
        result(i * (rows - HS), cols - HS, HS, HS)

    start(None, obuf.at[o], out.at[pl.ds(rows * f, rows)], OUT, partner)
    keep = pltpu.make_async_copy(obuf.at[f], out.at[pl.ds(rows * f, rows)], local.at[2])
    keep.start()
    landed(out.at[pl.ds(rows * o, rows)], OUT)
    keep.wait()
    for there, what in sends:
        if there is None:
            what.wait_send()
        else:
            @pl.when(there)
            def _(what=what):
                what.wait_send()


def solution(mesh):
    nrow, ncol = mesh.shape["row"], mesh.shape["col"]

    def per_device(grad_out, pre_act, weight_one, weight_two):
        batch, rows, cols, chan = grad_out.shape
        taps = lambda w: jnp.swapaxes(w, 2, 3).reshape(-1, w.shape[2])
        inward = lambda a: jnp.transpose(a, (1, 2, 0, 3))
        strip = rows // 2
        kind = grad_out.dtype
        out = pl.pallas_call(
            functools.partial(kernel, nrow, ncol),
            out_shape=jax.ShapeDtypeStruct((rows, cols, batch, chan), kind),
            in_specs=[pl.BlockSpec(memory_space=pl.ANY)] * 2 + [pl.BlockSpec(memory_space=pltpu.VMEM)] * 2,
            out_specs=pl.BlockSpec(memory_space=pl.ANY),
            scratch_shapes=[
                pltpu.VMEM((2, strip + 2 * GS, cols + 2 * GS, batch, chan), kind),
                pltpu.VMEM((2, strip, cols, batch, chan), kind),
                pltpu.VMEM((2, strip + 2 * HS, cols + 2 * HS, batch, chan), kind),
                pltpu.VMEM((2, strip, cols, batch, chan), kind),
                pltpu.VMEM((strip, GS, batch, chan), kind),
                pltpu.VMEM((2, strip, HS, batch, chan), kind),
                pltpu.SemaphoreType.DMA((30,)),
                pltpu.SemaphoreType.DMA((25,)),
                pltpu.SemaphoreType.DMA((3,)),
            ],
            compiler_params=pltpu.CompilerParams(
                collective_id=0, has_side_effects=True, vmem_limit_bytes=48 * 1024 * 1024),
            cost_estimate=pl.CostEstimate(
                flops=4 * 9 * batch * rows * cols * chan * 2 * chan, bytes_accessed=8 * batch * rows * cols * chan,
                transcendentals=0),
        )(inward(grad_out), inward(pre_act), taps(weight_one), taps(weight_two))
        return jnp.transpose(out, (2, 0, 1, 3))

    placed = (P(None, "row", "col", "filt"), P(None, "row", "col", "filt"), P(), P())
    return jax.shard_map(
        per_device, mesh=mesh, in_specs=placed, out_specs=P(None, "row", "col", "filt"), check_vma=False)
```

```python
import functools

import jax
import jax.numpy as jnp
from jax import lax
from jax.experimental import pallas as pl
from jax.experimental.pallas import tpu as pltpu
from jax.sharding import PartitionSpec as P

MESH = pl.DeviceIdType.MESH
GS = 4
HS = 2


def conv(buf, weight, row, col, rows, cols, spacing):
    batch = buf.shape[3]
    pieces = []
    for p in range(3):
        for q in range(3):
            for half in range(2):
                piece = buf[half, pl.ds(row + spacing * (2 - p), rows), pl.ds(col + spacing * (2 - q), cols)]
                pieces.append(piece.reshape(rows * cols * batch, piece.shape[-1]))
    return jnp.dot(jnp.concatenate(pieces, axis=1), weight[...], preferred_element_type=jnp.float32)


def kernel(nrow, ncol, g_in, p_in, k1, k2, out, gbuf, pbuf, hbuf, obuf, gvia, hvia, praw, w1, w2, send, recv, local):
    r, c, f = lax.axis_index("row"), lax.axis_index("col"), lax.axis_index("filt")
    o = 1 - f
    rows = g_in.shape[0] // 2
    cols = g_in.shape[1]
    batch, chan = g_in.shape[2], g_in.shape[3]
    has_left, has_right = c > 0, c < ncol - 1
    has_top, has_bot = r > 0, r < nrow - 1
    first, last = jnp.logical_and(f == 0, r == 0), jnp.logical_and(f == 1, r == nrow - 1)
    has_up, has_down = jnp.logical_not(first), jnp.logical_not(last)
    up = (r - o, c, o)
    down = (r + f, c, o)
    partner = (r, c, o)
    folded = ncol == 4
    across = lax.rem(c + 2, 4)

    @pl.when(first)
    def _():
        gbuf[:, :GS] = jnp.zeros((2, GS) + gbuf.shape[2:], gbuf.dtype)
        hbuf[:, :HS] = jnp.zeros((2, HS) + hbuf.shape[2:], hbuf.dtype)

    @pl.when(last)
    def _():
        gbuf[:, rows + GS:] = jnp.zeros((2, GS) + gbuf.shape[2:], gbuf.dtype)
        hbuf[:, rows + HS:] = jnp.zeros((2, HS) + hbuf.shape[2:], hbuf.dtype)

    @pl.when(jnp.logical_not(has_left))
    def _():
        gbuf[:, :, :GS] = jnp.zeros((2, rows + 2 * GS, GS, batch, chan), gbuf.dtype)
        hbuf[:, :, :HS] = jnp.zeros((2, rows + 2 * HS, HS, batch, chan), hbuf.dtype)

    @pl.when(jnp.logical_not(has_right))
    def _():
        gbuf[:, :, cols + GS:] = jnp.zeros((2, rows + 2 * GS, GS, batch, chan), gbuf.dtype)
        hbuf[:, :, cols + HS:] = jnp.zeros((2, rows + 2 * HS, HS, batch, chan), hbuf.dtype)

    barrier = pltpu.get_barrier_semaphore()
    pl.semaphore_signal(barrier, inc=1, device_id=partner, device_id_type=MESH)
    count = jnp.int32(1)
    for there, rr, cc in ((has_left, r, c - 1), (has_right, r, c + 1), (has_top, r - 1, c), (has_bot, r + 1, c)):
        @pl.when(there)
        def _(rr=rr, cc=cc):
            for ff in range(2):
                pl.semaphore_signal(barrier, inc=1, device_id=(rr, cc, ff), device_id_type=MESH)
        count = count + jnp.where(there, 2, 0)
    if folded:
        pl.semaphore_signal(barrier, inc=1, device_id=(r, across, f), device_id_type=MESH)
        count = count + 1
    pl.semaphore_wait(barrier, count)

    def copy(src, dst, sidx, ridx, device):
        return pltpu.make_async_remote_copy(
            src_ref=src, dst_ref=dst, send_sem=send.at[sidx], recv_sem=recv.at[ridx],
            device_id=device, device_id_type=MESH)

    def landed(dst, ridx):
        copy(dst, dst, 0, ridx, partner).wait_recv()

    sends = []

    def start(there, src, dst, ridx, device):
        sidx = len(sends)
        what = copy(src, dst, sidx, ridx, device)
        sends.append((there, what))
        if there is None:
            what.start()
        else:
            @pl.when(there)
            def _():
                what.start()

    grow, gcol = pl.ds(GS, rows), pl.ds(GS, cols)
    hrow, hcol = pl.ds(HS, rows), pl.ds(HS, cols)
    L, R, T, B, MAIN, PRE, CORNER, HL, HR, HT, HB, HCORNER, OUT, VIA, HVIA = (
        0, 2, 4, 6, 8, 9, 10, 14, 15, 16, 17, 18, 22, 23, 24)

    if folded:
        start(c == 1, g_in.at[pl.ds(rows, rows), pl.ds(cols - GS, GS)], gvia, VIA, (r, across, f))
        start(c == 2, g_in.at[pl.ds(rows, rows), pl.ds(0, GS)], gvia, VIA, (r, across, f))
    for ff in range(2):
        to_right, to_left = has_right, has_left
        if folded and ff == 1:
            to_right = jnp.logical_and(has_right, c != 1)
            to_left = jnp.logical_and(has_left, c != 2)
        start(to_right, g_in.at[pl.ds(rows * ff, rows), pl.ds(cols - GS, GS)], gbuf.at[f, grow, pl.ds(0, GS)],
              L + f, (r, c + 1, ff))
        start(to_left, g_in.at[pl.ds(rows * ff, rows), pl.ds(0, GS)], gbuf.at[f, grow, pl.ds(cols + GS, GS)],
              R + f, (r, c - 1, ff))
    span = rows + GS
    start(None, g_in.at[pl.ds((rows - GS) * o, span)], gbuf.at[f, pl.ds(GS * f, span), gcol], MAIN, partner)
    mine = pltpu.make_async_copy(
        g_in.at[pl.ds((rows - GS) * f, span)], gbuf.at[f, pl.ds(GS * o, span), gcol], local.at[0])
    mine.start()
    start(has_bot, g_in.at[pl.ds(2 * rows - GS, GS)], gbuf.at[f, pl.ds(0, GS), gcol], T + f, (r + 1, c, 0))
    start(has_top, g_in.at[pl.ds(0, GS)], gbuf.at[f, pl.ds(rows + GS, GS), gcol], B + f, (r - 1, c, 1))
    start(None, p_in.at[:, pl.ds(rows * o, rows)], praw.at[f], PRE, partner)
    own_pre = pltpu.make_async_copy(p_in.at[:, pl.ds(rows * f, rows)], praw.at[f], local.at[1])
    own_pre.start()

    for src, dst in ((k2, w2), (k1, w1)):
        depth = src.shape[3]
        for p in range(3):
            for q in range(3):
                dst[pl.ds((3 * p + q) * depth, depth)] = src[p, q].T

    if folded:
        @pl.when(jnp.logical_or(c == 0, c == 3))
        def _():
            landed(gvia, VIA)
        start(c == 3, gvia, gbuf.at[f, grow, pl.ds(0, GS)], L + f, (r, c - 1, 1))
        start(c == 0, gvia, gbuf.at[f, grow, pl.ds(cols + GS, GS)], R + f, (r, c + 1, 1))

    landed(gbuf.at[o, pl.ds(GS * o, span), gcol], MAIN)
    mine.wait()
    landed(praw.at[o], PRE)
    own_pre.wait()

    @pl.loop(0, rows)
    def _(y):
        for half in range(2):
            pbuf[half, y] = jnp.swapaxes(praw[half, :, y], 0, 1)

    @pl.when(jnp.logical_and(f == 0, has_top))
    def _():
        for half in range(2):
            landed(gbuf.at[half, pl.ds(0, GS), gcol], T + half)

    @pl.when(jnp.logical_and(f == 1, has_bot))
    def _():
        for half in range(2):
            landed(gbuf.at[half, pl.ds(rows + GS, GS), gcol], B + half)

    def hidden(row, col, nr, nc):
        total = conv(gbuf, w2, row, col, nr, nc, GS)
        for half in range(2):
            keep = pbuf[half, pl.ds(row, nr), pl.ds(col, nc)].reshape(nr * nc * batch, chan).astype(jnp.float32) > 0
            part = jnp.where(keep, total[:, half * chan:(half + 1) * chan], 0.0).astype(hbuf.dtype)
            hbuf[half, pl.ds(row + HS, nr), pl.ds(col + HS, nc)] = part.reshape(nr, nc, batch, chan)

    @pl.loop(0, rows // 4)
    def _(i):
        hidden(i * 4, GS, 4, cols - 2 * GS)

    @pl.when(has_left)
    def _():
        for half in range(2):
            landed(gbuf.at[half, grow, pl.ds(0, GS)], L + half)

    @pl.when(has_right)
    def _():
        for half in range(2):
            landed(gbuf.at[half, grow, pl.ds(cols + GS, GS)], R + half)

    both = pl.ds(0, 2)

    def corners(buf, width, size, base):
        for side, there, col in ((0, has_left, 0), (1, has_right, cols + width)):
            at = pl.ds(col, width)
            start(jnp.logical_and(there, has_up), buf.at[both, pl.ds(width, width), at],
                  buf.at[both, pl.ds(rows + width, width), at], base + side, up)
            start(jnp.logical_and(there, has_down), buf.at[both, pl.ds(rows, width), at],
                  buf.at[both, pl.ds(0, width), at], base + 2 + side, down)

    def corners_landed(buf, width, base):
        for side, there, col in ((0, has_left, 0), (1, has_right, cols + width)):
            at = pl.ds(col, width)

            @pl.when(jnp.logical_and(there, has_down))
            def _(side=side, at=at):
                landed(buf.at[both, pl.ds(rows + width, width), at], base + side)

            @pl.when(jnp.logical_and(there, has_up))
            def _(side=side, at=at):
                landed(buf.at[both, pl.ds(0, width), at], base + 2 + side)

    corners(gbuf, GS, GS, CORNER)

    @pl.loop(1, rows // 4 - 1)
    def _(i):
        hidden(i * 4, 0, 4, GS)
        hidden(i * 4, cols - GS, 4, GS)

    corners_landed(gbuf, GS, CORNER)

    @pl.loop(0, 2)
    def _(i):
        at = i * (rows - 4)
        hidden(at, 0, 4, GS)
        hidden(at, cols - GS, 4, GS)

    to_right, to_left = has_right, has_left
    if folded:
        start(jnp.logical_and(c == 1, f == 1), hbuf.at[both, hrow, pl.ds(cols, HS)], hvia, HVIA, (r, across, f))
        start(jnp.logical_and(c == 2, f == 1), hbuf.at[both, hrow, pl.ds(HS, HS)], hvia, HVIA, (r, across, f))
        to_right = jnp.logical_and(has_right, jnp.logical_or(c != 1, f == 0))
        to_left = jnp.logical_and(has_left, jnp.logical_or(c != 2, f == 0))
    start(to_right, hbuf.at[both, hrow, pl.ds(cols, HS)], hbuf.at[both, hrow, pl.ds(0, HS)], HL, (r, c + 1, f))
    start(to_left, hbuf.at[both, hrow, pl.ds(HS, HS)], hbuf.at[both, hrow, pl.ds(cols + HS, HS)], HR, (r, c - 1, f))
    start(has_up, hbuf.at[both, pl.ds(HS, HS), hcol], hbuf.at[both, pl.ds(rows + HS, HS), hcol], HB, up)
    start(has_down, hbuf.at[both, pl.ds(rows, HS), hcol], hbuf.at[both, pl.ds(0, HS), hcol], HT, down)

    def result(row, col, nr, nc):
        total = conv(hbuf, w1, row, col, nr, nc, HS)
        for half in range(2):
            part = total[:, half * chan:(half + 1) * chan].astype(obuf.dtype)
            obuf[half, pl.ds(row, nr), pl.ds(col, nc)] = part.reshape(nr, nc, batch, chan)

    @pl.loop(0, (rows - 2 * HS) // 4)
    def _(i):
        result(HS + i * 4, HS, 4, cols - 2 * HS)

    if folded:
        @pl.when(jnp.logical_and(jnp.logical_or(c == 0, c == 3), f == 1))
        def _():
            landed(hvia, HVIA)
        start(jnp.logical_and(c == 3, f == 1), hvia, hbuf.at[both, hrow, pl.ds(0, HS)], HL, (r, c - 1, f))
        start(jnp.logical_and(c == 0, f == 1), hvia, hbuf.at[both, hrow, pl.ds(cols + HS, HS)], HR, (r, c + 1, f))

    @pl.when(has_up)
    def _():
        landed(hbuf.at[both, pl.ds(0, HS), hcol], HT)

    @pl.when(has_down)
    def _():
        landed(hbuf.at[both, pl.ds(rows + HS, HS), hcol], HB)

    @pl.loop(0, 2)
    def _(i):
        result(i * (rows - HS), HS, HS, cols - 2 * HS)

    @pl.when(has_left)
    def _():
        landed(hbuf.at[both, hrow, pl.ds(0, HS)], HL)

    @pl.when(has_right)
    def _():
        landed(hbuf.at[both, hrow, pl.ds(cols + HS, HS)], HR)

    corners(hbuf, HS, HS, HCORNER)

    @pl.loop(0, 2)
    def _(i):
        result(HS, i * (cols - HS), rows - 2 * HS, HS)

    corners_landed(hbuf, HS, HCORNER)

    @pl.loop(0, 2)
    def _(i):
        result(i * (rows - HS), 0, HS, HS)
        result(i * (rows - HS), cols - HS, HS, HS)

    start(None, obuf.at[o], out.at[pl.ds(rows * f, rows)], OUT, partner)
    keep = pltpu.make_async_copy(obuf.at[f], out.at[pl.ds(rows * f, rows)], local.at[2])
    keep.start()
    landed(out.at[pl.ds(rows * o, rows)], OUT)
    keep.wait()
    for there, what in sends:
        if there is None:
            what.wait_send()
        else:
            @pl.when(there)
            def _(what=what):
                what.wait_send()


def solution(mesh):
    nrow, ncol = mesh.shape["row"], mesh.shape["col"]

    def per_device(grad_out, pre_act, weight_one, weight_two):
        batch, rows, cols, chan = grad_out.shape
        inward = lambda a: jnp.transpose(a, (1, 2, 0, 3))
        strip = rows // 2
        kind = grad_out.dtype
        out = pl.pallas_call(
            functools.partial(kernel, nrow, ncol),
            out_shape=jax.ShapeDtypeStruct((rows, cols, batch, chan), kind),
            in_specs=[pl.BlockSpec(memory_space=pl.ANY)] * 2 + [pl.BlockSpec(memory_space=pltpu.VMEM)] * 2,
            out_specs=pl.BlockSpec(memory_space=pl.ANY),
            scratch_shapes=[
                pltpu.VMEM((2, strip + 2 * GS, cols + 2 * GS, batch, chan), kind),
                pltpu.VMEM((2, strip, cols, batch, chan), kind),
                pltpu.VMEM((2, strip + 2 * HS, cols + 2 * HS, batch, chan), kind),
                pltpu.VMEM((2, strip, cols, batch, chan), kind),
                pltpu.VMEM((strip, GS, batch, chan), kind),
                pltpu.VMEM((2, strip, HS, batch, chan), kind),
                pltpu.VMEM((2, batch, strip, cols, chan), kind),
                pltpu.VMEM((9 * 2 * chan, 2 * chan), kind),
                pltpu.VMEM((9 * 2 * chan, 2 * chan), kind),
                pltpu.SemaphoreType.DMA((30,)),
                pltpu.SemaphoreType.DMA((25,)),
                pltpu.SemaphoreType.DMA((3,)),
            ],
            compiler_params=pltpu.CompilerParams(
                collective_id=0, has_side_effects=True, vmem_limit_bytes=48 * 1024 * 1024),
            cost_estimate=pl.CostEstimate(
                flops=4 * 9 * batch * rows * cols * chan * 2 * chan, bytes_accessed=8 * batch * rows * cols * chan,
                transcendentals=0),
        )(inward(grad_out), pre_act, weight_one, weight_two)
        return jnp.transpose(out, (2, 0, 1, 3))

    placed = (P(None, "row", "col", "filt"), P(None, "row", "col", "filt"), P(), P())
    return jax.shard_map(
        per_device, mesh=mesh, in_specs=placed, out_specs=P(None, "row", "col", "filt"), check_vma=False)
```

```python
import functools

import jax
import jax.numpy as jnp
from jax import lax
from jax.experimental import pallas as pl
from jax.experimental.pallas import tpu as pltpu
from jax.sharding import PartitionSpec as P

MESH = pl.DeviceIdType.MESH
GS = 4
HS = 2


def conv(buf, weight, row, col, rows, cols, spacing):
    batch = buf.shape[3]
    pieces = []
    for p in range(3):
        for q in range(3):
            for half in range(2):
                piece = buf[half, pl.ds(row + spacing * (2 - p), rows), pl.ds(col + spacing * (2 - q), cols)]
                pieces.append(piece.reshape(rows * cols * batch, piece.shape[-1]))
    return jnp.dot(jnp.concatenate(pieces, axis=1), weight[...], preferred_element_type=jnp.float32)


def kernel(nrow, ncol, g_raw, p_in, k1, k2, out, gbuf, pbuf, hbuf, obuf, gvia, hvia, praw, g_in, w1, w2, send, recv, local):
    r, c, f = lax.axis_index("row"), lax.axis_index("col"), lax.axis_index("filt")
    o = 1 - f
    rows = g_in.shape[0] // 2
    cols = g_in.shape[1]
    batch, chan = g_in.shape[2], g_in.shape[3]
    has_left, has_right = c > 0, c < ncol - 1
    has_top, has_bot = r > 0, r < nrow - 1
    first, last = jnp.logical_and(f == 0, r == 0), jnp.logical_and(f == 1, r == nrow - 1)
    has_up, has_down = jnp.logical_not(first), jnp.logical_not(last)
    up = (r - o, c, o)
    down = (r + f, c, o)
    partner = (r, c, o)
    folded = ncol == 4
    across = lax.rem(c + 2, 4)

    @pl.when(first)
    def _():
        gbuf[:, :GS] = jnp.zeros((2, GS) + gbuf.shape[2:], gbuf.dtype)
        hbuf[:, :HS] = jnp.zeros((2, HS) + hbuf.shape[2:], hbuf.dtype)

    @pl.when(last)
    def _():
        gbuf[:, rows + GS:] = jnp.zeros((2, GS) + gbuf.shape[2:], gbuf.dtype)
        hbuf[:, rows + HS:] = jnp.zeros((2, HS) + hbuf.shape[2:], hbuf.dtype)

    @pl.when(jnp.logical_not(has_left))
    def _():
        gbuf[:, :, :GS] = jnp.zeros((2, rows + 2 * GS, GS, batch, chan), gbuf.dtype)
        hbuf[:, :, :HS] = jnp.zeros((2, rows + 2 * HS, HS, batch, chan), hbuf.dtype)

    @pl.when(jnp.logical_not(has_right))
    def _():
        gbuf[:, :, cols + GS:] = jnp.zeros((2, rows + 2 * GS, GS, batch, chan), gbuf.dtype)
        hbuf[:, :, cols + HS:] = jnp.zeros((2, rows + 2 * HS, HS, batch, chan), hbuf.dtype)

    barrier = pltpu.get_barrier_semaphore()
    pl.semaphore_signal(barrier, inc=1, device_id=partner, device_id_type=MESH)
    count = jnp.int32(1)
    for there, rr, cc in ((has_left, r, c - 1), (has_right, r, c + 1), (has_top, r - 1, c), (has_bot, r + 1, c)):
        @pl.when(there)
        def _(rr=rr, cc=cc):
            for ff in range(2):
                pl.semaphore_signal(barrier, inc=1, device_id=(rr, cc, ff), device_id_type=MESH)
        count = count + jnp.where(there, 2, 0)
    if folded:
        pl.semaphore_signal(barrier, inc=1, device_id=(r, across, f), device_id_type=MESH)
        count = count + 1

    @pl.loop(0, 2 * rows)
    def _(y):
        g_in[y] = jnp.swapaxes(g_raw[:, y], 0, 1)

    pl.semaphore_wait(barrier, count)

    def copy(src, dst, sidx, ridx, device):
        return pltpu.make_async_remote_copy(
            src_ref=src, dst_ref=dst, send_sem=send.at[sidx], recv_sem=recv.at[ridx],
            device_id=device, device_id_type=MESH)

    def landed(dst, ridx):
        copy(dst, dst, 0, ridx, partner).wait_recv()

    sends = []

    def start(there, src, dst, ridx, device):
        sidx = len(sends)
        what = copy(src, dst, sidx, ridx, device)
        sends.append((there, what))
        if there is None:
            what.start()
        else:
            @pl.when(there)
            def _():
                what.start()

    grow, gcol = pl.ds(GS, rows), pl.ds(GS, cols)
    hrow, hcol = pl.ds(HS, rows), pl.ds(HS, cols)
    L, R, T, B, MAIN, PRE, CORNER, HL, HR, HT, HB, HCORNER, OUT, VIA, HVIA = (
        0, 2, 4, 6, 8, 9, 10, 14, 15, 16, 17, 18, 22, 23, 24)

    if folded:
        start(c == 1, g_in.at[pl.ds(rows, rows), pl.ds(cols - GS, GS)], gvia, VIA, (r, across, f))
        start(c == 2, g_in.at[pl.ds(rows, rows), pl.ds(0, GS)], gvia, VIA, (r, across, f))
    for ff in range(2):
        to_right, to_left = has_right, has_left
        if folded and ff == 1:
            to_right = jnp.logical_and(has_right, c != 1)
            to_left = jnp.logical_and(has_left, c != 2)
        start(to_right, g_in.at[pl.ds(rows * ff, rows), pl.ds(cols - GS, GS)], gbuf.at[f, grow, pl.ds(0, GS)],
              L + f, (r, c + 1, ff))
        start(to_left, g_in.at[pl.ds(rows * ff, rows), pl.ds(0, GS)], gbuf.at[f, grow, pl.ds(cols + GS, GS)],
              R + f, (r, c - 1, ff))
    span = rows + GS
    start(None, g_in.at[pl.ds((rows - GS) * o, span)], gbuf.at[f, pl.ds(GS * f, span), gcol], MAIN, partner)
    mine = pltpu.make_async_copy(
        g_in.at[pl.ds((rows - GS) * f, span)], gbuf.at[f, pl.ds(GS * o, span), gcol], local.at[0])
    mine.start()
    start(has_bot, g_in.at[pl.ds(2 * rows - GS, GS)], gbuf.at[f, pl.ds(0, GS), gcol], T + f, (r + 1, c, 0))
    start(has_top, g_in.at[pl.ds(0, GS)], gbuf.at[f, pl.ds(rows + GS, GS), gcol], B + f, (r - 1, c, 1))
    start(None, p_in.at[:, pl.ds(rows * o, rows)], praw.at[f], PRE, partner)
    own_pre = pltpu.make_async_copy(p_in.at[:, pl.ds(rows * f, rows)], praw.at[f], local.at[1])
    own_pre.start()

    for src, dst in ((k2, w2), (k1, w1)):
        depth = src.shape[3]
        for p in range(3):
            for q in range(3):
                dst[pl.ds((3 * p + q) * depth, depth)] = src[p, q].T

    if folded:
        @pl.when(jnp.logical_or(c == 0, c == 3))
        def _():
            landed(gvia, VIA)
        start(c == 3, gvia, gbuf.at[f, grow, pl.ds(0, GS)], L + f, (r, c - 1, 1))
        start(c == 0, gvia, gbuf.at[f, grow, pl.ds(cols + GS, GS)], R + f, (r, c + 1, 1))

    landed(gbuf.at[o, pl.ds(GS * o, span), gcol], MAIN)
    mine.wait()
    landed(praw.at[o], PRE)
    own_pre.wait()

    @pl.loop(0, rows)
    def _(y):
        for half in range(2):
            pbuf[half, y] = jnp.swapaxes(praw[half, :, y], 0, 1)

    @pl.when(jnp.logical_and(f == 0, has_top))
    def _():
        for half in range(2):
            landed(gbuf.at[half, pl.ds(0, GS), gcol], T + half)

    @pl.when(jnp.logical_and(f == 1, has_bot))
    def _():
        for half in range(2):
            landed(gbuf.at[half, pl.ds(rows + GS, GS), gcol], B + half)

    def hidden(row, col, nr, nc):
        total = conv(gbuf, w2, row, col, nr, nc, GS)
        for half in range(2):
            keep = pbuf[half, pl.ds(row, nr), pl.ds(col, nc)].reshape(nr * nc * batch, chan).astype(jnp.float32) > 0
            part = jnp.where(keep, total[:, half * chan:(half + 1) * chan], 0.0).astype(hbuf.dtype)
            hbuf[half, pl.ds(row + HS, nr), pl.ds(col + HS, nc)] = part.reshape(nr, nc, batch, chan)

    @pl.loop(0, rows // 4)
    def _(i):
        hidden(i * 4, GS, 4, cols - 2 * GS)

    @pl.when(has_left)
    def _():
        for half in range(2):
            landed(gbuf.at[half, grow, pl.ds(0, GS)], L + half)

    @pl.when(has_right)
    def _():
        for half in range(2):
            landed(gbuf.at[half, grow, pl.ds(cols + GS, GS)], R + half)

    both = pl.ds(0, 2)

    def corners(buf, width, size, base):
        for side, there, col in ((0, has_left, 0), (1, has_right, cols + width)):
            at = pl.ds(col, width)
            start(jnp.logical_and(there, has_up), buf.at[both, pl.ds(width, width), at],
                  buf.at[both, pl.ds(rows + width, width), at], base + side, up)
            start(jnp.logical_and(there, has_down), buf.at[both, pl.ds(rows, width), at],
                  buf.at[both, pl.ds(0, width), at], base + 2 + side, down)

    def corners_landed(buf, width, base):
        for side, there, col in ((0, has_left, 0), (1, has_right, cols + width)):
            at = pl.ds(col, width)

            @pl.when(jnp.logical_and(there, has_down))
            def _(side=side, at=at):
                landed(buf.at[both, pl.ds(rows + width, width), at], base + side)

            @pl.when(jnp.logical_and(there, has_up))
            def _(side=side, at=at):
                landed(buf.at[both, pl.ds(0, width), at], base + 2 + side)

    corners(gbuf, GS, GS, CORNER)

    @pl.loop(1, rows // 4 - 1)
    def _(i):
        hidden(i * 4, 0, 4, GS)
        hidden(i * 4, cols - GS, 4, GS)

    corners_landed(gbuf, GS, CORNER)

    @pl.loop(0, 2)
    def _(i):
        at = i * (rows - 4)
        hidden(at, 0, 4, GS)
        hidden(at, cols - GS, 4, GS)

    to_right, to_left = has_right, has_left
    if folded:
        start(jnp.logical_and(c == 1, f == 1), hbuf.at[both, hrow, pl.ds(cols, HS)], hvia, HVIA, (r, across, f))
        start(jnp.logical_and(c == 2, f == 1), hbuf.at[both, hrow, pl.ds(HS, HS)], hvia, HVIA, (r, across, f))
        to_right = jnp.logical_and(has_right, jnp.logical_or(c != 1, f == 0))
        to_left = jnp.logical_and(has_left, jnp.logical_or(c != 2, f == 0))
    start(to_right, hbuf.at[both, hrow, pl.ds(cols, HS)], hbuf.at[both, hrow, pl.ds(0, HS)], HL, (r, c + 1, f))
    start(to_left, hbuf.at[both, hrow, pl.ds(HS, HS)], hbuf.at[both, hrow, pl.ds(cols + HS, HS)], HR, (r, c - 1, f))
    start(has_up, hbuf.at[both, pl.ds(HS, HS), hcol], hbuf.at[both, pl.ds(rows + HS, HS), hcol], HB, up)
    start(has_down, hbuf.at[both, pl.ds(rows, HS), hcol], hbuf.at[both, pl.ds(0, HS), hcol], HT, down)

    def result(row, col, nr, nc):
        total = conv(hbuf, w1, row, col, nr, nc, HS)
        for half in range(2):
            part = total[:, half * chan:(half + 1) * chan].astype(obuf.dtype)
            obuf[half, pl.ds(row, nr), pl.ds(col, nc)] = part.reshape(nr, nc, batch, chan)

    @pl.loop(0, (rows - 2 * HS) // 4)
    def _(i):
        result(HS + i * 4, HS, 4, cols - 2 * HS)

    if folded:
        @pl.when(jnp.logical_and(jnp.logical_or(c == 0, c == 3), f == 1))
        def _():
            landed(hvia, HVIA)
        start(jnp.logical_and(c == 3, f == 1), hvia, hbuf.at[both, hrow, pl.ds(0, HS)], HL, (r, c - 1, f))
        start(jnp.logical_and(c == 0, f == 1), hvia, hbuf.at[both, hrow, pl.ds(cols + HS, HS)], HR, (r, c + 1, f))

    @pl.when(has_up)
    def _():
        landed(hbuf.at[both, pl.ds(0, HS), hcol], HT)

    @pl.when(has_down)
    def _():
        landed(hbuf.at[both, pl.ds(rows + HS, HS), hcol], HB)

    @pl.loop(0, 2)
    def _(i):
        result(i * (rows - HS), HS, HS, cols - 2 * HS)

    @pl.when(has_left)
    def _():
        landed(hbuf.at[both, hrow, pl.ds(0, HS)], HL)

    @pl.when(has_right)
    def _():
        landed(hbuf.at[both, hrow, pl.ds(cols + HS, HS)], HR)

    corners(hbuf, HS, HS, HCORNER)

    @pl.loop(0, 2)
    def _(i):
        result(HS, i * (cols - HS), rows - 2 * HS, HS)

    corners_landed(hbuf, HS, HCORNER)

    @pl.loop(0, 2)
    def _(i):
        result(i * (rows - HS), 0, HS, HS)
        result(i * (rows - HS), cols - HS, HS, HS)

    start(None, obuf.at[o], out.at[pl.ds(rows * f, rows)], OUT, partner)
    keep = pltpu.make_async_copy(obuf.at[f], out.at[pl.ds(rows * f, rows)], local.at[2])
    keep.start()
    landed(out.at[pl.ds(rows * o, rows)], OUT)
    keep.wait()
    for there, what in sends:
        if there is None:
            what.wait_send()
        else:
            @pl.when(there)
            def _(what=what):
                what.wait_send()


def solution(mesh):
    nrow, ncol = mesh.shape["row"], mesh.shape["col"]

    def per_device(grad_out, pre_act, weight_one, weight_two):
        batch, rows, cols, chan = grad_out.shape
        strip = rows // 2
        kind = grad_out.dtype
        out = pl.pallas_call(
            functools.partial(kernel, nrow, ncol),
            out_shape=jax.ShapeDtypeStruct((rows, cols, batch, chan), kind),
            in_specs=[pl.BlockSpec(memory_space=pltpu.VMEM), pl.BlockSpec(memory_space=pl.ANY)] + [pl.BlockSpec(memory_space=pltpu.VMEM)] * 2,
            out_specs=pl.BlockSpec(memory_space=pl.ANY),
            scratch_shapes=[
                pltpu.VMEM((2, strip + 2 * GS, cols + 2 * GS, batch, chan), kind),
                pltpu.VMEM((2, strip, cols, batch, chan), kind),
                pltpu.VMEM((2, strip + 2 * HS, cols + 2 * HS, batch, chan), kind),
                pltpu.VMEM((2, strip, cols, batch, chan), kind),
                pltpu.VMEM((strip, GS, batch, chan), kind),
                pltpu.VMEM((2, strip, HS, batch, chan), kind),
                pltpu.VMEM((2, batch, strip, cols, chan), kind),
                pltpu.VMEM((rows, cols, batch, chan), kind),
                pltpu.VMEM((9 * 2 * chan, 2 * chan), kind),
                pltpu.VMEM((9 * 2 * chan, 2 * chan), kind),
                pltpu.SemaphoreType.DMA((30,)),
                pltpu.SemaphoreType.DMA((25,)),
                pltpu.SemaphoreType.DMA((3,)),
            ],
            compiler_params=pltpu.CompilerParams(
                collective_id=0, has_side_effects=True, vmem_limit_bytes=48 * 1024 * 1024),
            cost_estimate=pl.CostEstimate(
                flops=4 * 9 * batch * rows * cols * chan * 2 * chan, bytes_accessed=8 * batch * rows * cols * chan,
                transcendentals=0),
        )(grad_out, pre_act, weight_one, weight_two)
        return jnp.transpose(out, (2, 0, 1, 3))

    placed = (P(None, "row", "col", "filt"), P(None, "row", "col", "filt"), P(), P())
    return jax.shard_map(
        per_device, mesh=mesh, in_specs=placed, out_specs=P(None, "row", "col", "filt"), check_vma=False)
```

```python
import functools

import jax
import jax.numpy as jnp
from jax import lax
from jax.experimental import pallas as pl
from jax.experimental.pallas import tpu as pltpu
from jax.sharding import PartitionSpec as P

MESH = pl.DeviceIdType.MESH
GS = 4
HS = 2


def conv(buf, weight, row, col, rows, cols, spacing):
    batch = buf.shape[3]
    pieces = []
    for p in range(3):
        for q in range(3):
            for half in range(2):
                piece = buf[half, pl.ds(row + spacing * (2 - p), rows), pl.ds(col + spacing * (2 - q), cols)]
                pieces.append(piece.reshape(rows * cols * batch, piece.shape[-1]))
    return jnp.dot(jnp.concatenate(pieces, axis=1), weight[...], preferred_element_type=jnp.float32)


def kernel(nrow, ncol, g_raw, p_in, k1, k2, out, gbuf, pbuf, hbuf, obuf, gvia, hvia, praw, g_in, w1, w2, send, recv, local):
    r, c, f = lax.axis_index("row"), lax.axis_index("col"), lax.axis_index("filt")
    o = 1 - f
    rows = g_in.shape[0] // 2
    cols = g_in.shape[1]
    batch, chan = g_in.shape[2], g_in.shape[3]
    has_left, has_right = c > 0, c < ncol - 1
    has_top, has_bot = r > 0, r < nrow - 1
    first, last = jnp.logical_and(f == 0, r == 0), jnp.logical_and(f == 1, r == nrow - 1)
    has_up, has_down = jnp.logical_not(first), jnp.logical_not(last)
    up = (r - o, c, o)
    down = (r + f, c, o)
    partner = (r, c, o)
    folded = ncol == 4
    across = lax.rem(c + 2, 4)

    @pl.when(first)
    def _():
        gbuf[:, :GS] = jnp.zeros((2, GS) + gbuf.shape[2:], gbuf.dtype)
        hbuf[:, :HS] = jnp.zeros((2, HS) + hbuf.shape[2:], hbuf.dtype)

    @pl.when(last)
    def _():
        gbuf[:, rows + GS:] = jnp.zeros((2, GS) + gbuf.shape[2:], gbuf.dtype)
        hbuf[:, rows + HS:] = jnp.zeros((2, HS) + hbuf.shape[2:], hbuf.dtype)

    @pl.when(jnp.logical_not(has_left))
    def _():
        gbuf[:, :, :GS] = jnp.zeros((2, rows + 2 * GS, GS, batch, chan), gbuf.dtype)
        hbuf[:, :, :HS] = jnp.zeros((2, rows + 2 * HS, HS, batch, chan), hbuf.dtype)

    @pl.when(jnp.logical_not(has_right))
    def _():
        gbuf[:, :, cols + GS:] = jnp.zeros((2, rows + 2 * GS, GS, batch, chan), gbuf.dtype)
        hbuf[:, :, cols + HS:] = jnp.zeros((2, rows + 2 * HS, HS, batch, chan), hbuf.dtype)

    barrier = pltpu.get_barrier_semaphore()
    pl.semaphore_signal(barrier, inc=1, device_id=partner, device_id_type=MESH)
    count = jnp.int32(1)
    for there, rr, cc in ((has_left, r, c - 1), (has_right, r, c + 1), (has_top, r - 1, c), (has_bot, r + 1, c)):
        @pl.when(there)
        def _(rr=rr, cc=cc):
            for ff in range(2):
                pl.semaphore_signal(barrier, inc=1, device_id=(rr, cc, ff), device_id_type=MESH)
        count = count + jnp.where(there, 2, 0)
    if folded:
        pl.semaphore_signal(barrier, inc=1, device_id=(r, across, f), device_id_type=MESH)
        count = count + 1

    @pl.loop(0, 2 * rows)
    def _(y):
        g_in[y] = jnp.swapaxes(g_raw[:, y], 0, 1)

    pl.semaphore_wait(barrier, count)

    def copy(src, dst, sidx, ridx, device):
        return pltpu.make_async_remote_copy(
            src_ref=src, dst_ref=dst, send_sem=send.at[sidx], recv_sem=recv.at[ridx],
            device_id=device, device_id_type=MESH)

    def landed(dst, ridx):
        copy(dst, dst, 0, ridx, partner).wait_recv()

    sends = []

    def start(there, src, dst, ridx, device):
        sidx = len(sends)
        what = copy(src, dst, sidx, ridx, device)
        sends.append((there, what))
        if there is None:
            what.start()
        else:
            @pl.when(there)
            def _():
                what.start()

    grow, gcol = pl.ds(GS, rows), pl.ds(GS, cols)
    hrow, hcol = pl.ds(HS, rows), pl.ds(HS, cols)
    L, R, T, B, MAIN, PRE, CORNER, HL, HR, HT, HB, HCORNER, OUT, VIA, HVIA = (
        0, 2, 4, 6, 8, 9, 10, 14, 15, 16, 17, 18, 22, 23, 24)
    OUTS = (OUT, 25, 26)

    if folded:
        start(c == 1, g_in.at[pl.ds(rows, rows), pl.ds(cols - GS, GS)], gvia, VIA, (r, across, f))
        start(c == 2, g_in.at[pl.ds(rows, rows), pl.ds(0, GS)], gvia, VIA, (r, across, f))
    for ff in range(2):
        to_right, to_left = has_right, has_left
        if folded and ff == 1:
            to_right = jnp.logical_and(has_right, c != 1)
            to_left = jnp.logical_and(has_left, c != 2)
        start(to_right, g_in.at[pl.ds(rows * ff, rows), pl.ds(cols - GS, GS)], gbuf.at[f, grow, pl.ds(0, GS)],
              L + f, (r, c + 1, ff))
        start(to_left, g_in.at[pl.ds(rows * ff, rows), pl.ds(0, GS)], gbuf.at[f, grow, pl.ds(cols + GS, GS)],
              R + f, (r, c - 1, ff))
    span = rows + GS
    start(None, g_in.at[pl.ds((rows - GS) * o, span)], gbuf.at[f, pl.ds(GS * f, span), gcol], MAIN, partner)
    mine = pltpu.make_async_copy(
        g_in.at[pl.ds((rows - GS) * f, span)], gbuf.at[f, pl.ds(GS * o, span), gcol], local.at[0])
    mine.start()
    start(has_bot, g_in.at[pl.ds(2 * rows - GS, GS)], gbuf.at[f, pl.ds(0, GS), gcol], T + f, (r + 1, c, 0))
    start(has_top, g_in.at[pl.ds(0, GS)], gbuf.at[f, pl.ds(rows + GS, GS), gcol], B + f, (r - 1, c, 1))
    start(None, p_in.at[:, pl.ds(rows * o, rows)], praw.at[f], PRE, partner)
    own_pre = pltpu.make_async_copy(p_in.at[:, pl.ds(rows * f, rows)], praw.at[f], local.at[1])
    own_pre.start()

    for src, dst in ((k2, w2), (k1, w1)):
        depth = src.shape[3]
        for p in range(3):
            for q in range(3):
                dst[pl.ds((3 * p + q) * depth, depth)] = src[p, q].T

    if folded:
        @pl.when(jnp.logical_or(c == 0, c == 3))
        def _():
            landed(gvia, VIA)
        start(c == 3, gvia, gbuf.at[f, grow, pl.ds(0, GS)], L + f, (r, c - 1, 1))
        start(c == 0, gvia, gbuf.at[f, grow, pl.ds(cols + GS, GS)], R + f, (r, c + 1, 1))

    landed(gbuf.at[o, pl.ds(GS * o, span), gcol], MAIN)
    mine.wait()
    landed(praw.at[o], PRE)
    own_pre.wait()

    @pl.loop(0, rows)
    def _(y):
        for half in range(2):
            pbuf[half, y] = jnp.swapaxes(praw[half, :, y], 0, 1)

    @pl.when(jnp.logical_and(f == 0, has_top))
    def _():
        for half in range(2):
            landed(gbuf.at[half, pl.ds(0, GS), gcol], T + half)

    @pl.when(jnp.logical_and(f == 1, has_bot))
    def _():
        for half in range(2):
            landed(gbuf.at[half, pl.ds(rows + GS, GS), gcol], B + half)

    def hidden(row, col, nr, nc):
        total = conv(gbuf, w2, row, col, nr, nc, GS)
        for half in range(2):
            keep = pbuf[half, pl.ds(row, nr), pl.ds(col, nc)].reshape(nr * nc * batch, chan).astype(jnp.float32) > 0
            part = jnp.where(keep, total[:, half * chan:(half + 1) * chan], 0.0).astype(hbuf.dtype)
            hbuf[half, pl.ds(row + HS, nr), pl.ds(col + HS, nc)] = part.reshape(nr, nc, batch, chan)

    @pl.loop(0, rows // 4)
    def _(i):
        hidden(i * 4, GS, 4, cols - 2 * GS)

    @pl.when(has_left)
    def _():
        for half in range(2):
            landed(gbuf.at[half, grow, pl.ds(0, GS)], L + half)

    @pl.when(has_right)
    def _():
        for half in range(2):
            landed(gbuf.at[half, grow, pl.ds(cols + GS, GS)], R + half)

    both = pl.ds(0, 2)

    def corners(buf, width, size, base):
        for side, there, col in ((0, has_left, 0), (1, has_right, cols + width)):
            at = pl.ds(col, width)
            start(jnp.logical_and(there, has_up), buf.at[both, pl.ds(width, width), at],
                  buf.at[both, pl.ds(rows + width, width), at], base + side, up)
            start(jnp.logical_and(there, has_down), buf.at[both, pl.ds(rows, width), at],
                  buf.at[both, pl.ds(0, width), at], base + 2 + side, down)

    def corners_landed(buf, width, base):
        for side, there, col in ((0, has_left, 0), (1, has_right, cols + width)):
            at = pl.ds(col, width)

            @pl.when(jnp.logical_and(there, has_down))
            def _(side=side, at=at):
                landed(buf.at[both, pl.ds(rows + width, width), at], base + side)

            @pl.when(jnp.logical_and(there, has_up))
            def _(side=side, at=at):
                landed(buf.at[both, pl.ds(0, width), at], base + 2 + side)

    corners(gbuf, GS, GS, CORNER)

    @pl.loop(1, rows // 4 - 1)
    def _(i):
        hidden(i * 4, 0, 4, GS)
        hidden(i * 4, cols - GS, 4, GS)

    corners_landed(gbuf, GS, CORNER)

    @pl.loop(0, 2)
    def _(i):
        at = i * (rows - 4)
        hidden(at, 0, 4, GS)
        hidden(at, cols - GS, 4, GS)

    to_right, to_left = has_right, has_left
    if folded:
        start(jnp.logical_and(c == 1, f == 1), hbuf.at[both, hrow, pl.ds(cols, HS)], hvia, HVIA, (r, across, f))
        start(jnp.logical_and(c == 2, f == 1), hbuf.at[both, hrow, pl.ds(HS, HS)], hvia, HVIA, (r, across, f))
        to_right = jnp.logical_and(has_right, jnp.logical_or(c != 1, f == 0))
        to_left = jnp.logical_and(has_left, jnp.logical_or(c != 2, f == 0))
    start(to_right, hbuf.at[both, hrow, pl.ds(cols, HS)], hbuf.at[both, hrow, pl.ds(0, HS)], HL, (r, c + 1, f))
    start(to_left, hbuf.at[both, hrow, pl.ds(HS, HS)], hbuf.at[both, hrow, pl.ds(cols + HS, HS)], HR, (r, c - 1, f))
    start(has_up, hbuf.at[both, pl.ds(HS, HS), hcol], hbuf.at[both, pl.ds(rows + HS, HS), hcol], HB, up)
    start(has_down, hbuf.at[both, pl.ds(rows, HS), hcol], hbuf.at[both, pl.ds(0, HS), hcol], HT, down)

    def result(row, col, nr, nc):
        total = conv(hbuf, w1, row, col, nr, nc, HS)
        for half in range(2):
            part = total[:, half * chan:(half + 1) * chan].astype(obuf.dtype)
            obuf[half, pl.ds(row, nr), pl.ds(col, nc)] = part.reshape(nr, nc, batch, chan)

    @pl.loop(0, (rows - 2 * HS) // 4)
    def _(i):
        result(HS + i * 4, HS, 4, cols - 2 * HS)

    if folded:
        @pl.when(jnp.logical_and(jnp.logical_or(c == 0, c == 3), f == 1))
        def _():
            landed(hvia, HVIA)
        start(jnp.logical_and(c == 3, f == 1), hvia, hbuf.at[both, hrow, pl.ds(0, HS)], HL, (r, c - 1, f))
        start(jnp.logical_and(c == 0, f == 1), hvia, hbuf.at[both, hrow, pl.ds(cols + HS, HS)], HR, (r, c + 1, f))

    @pl.when(has_up)
    def _():
        landed(hbuf.at[both, pl.ds(0, HS), hcol], HT)

    @pl.when(has_down)
    def _():
        landed(hbuf.at[both, pl.ds(rows + HS, HS), hcol], HB)

    @pl.loop(0, 2)
    def _(i):
        result(i * (rows - HS), HS, HS, cols - 2 * HS)

    given = []

    def deliver(part, col, nc):
        at = pl.ds(col, nc)
        own = out.at[pl.ds(rows * f, rows), at]
        ridx = OUTS[part]
        start(None, obuf.at[o, pl.ds(0, rows), at], own, ridx, partner)
        keep = pltpu.make_async_copy(obuf.at[f, pl.ds(0, rows), at], own, local.at[2 + part])
        keep.start()
        given.append((keep, out.at[pl.ds(rows * o, rows), at], ridx))

    deliver(0, HS, cols - 2 * HS)

    @pl.when(has_left)
    def _():
        landed(hbuf.at[both, hrow, pl.ds(0, HS)], HL)

    @pl.when(has_right)
    def _():
        landed(hbuf.at[both, hrow, pl.ds(cols + HS, HS)], HR)

    corners(hbuf, HS, HS, HCORNER)

    @pl.loop(0, 2)
    def _(i):
        result(HS, i * (cols - HS), rows - 2 * HS, HS)

    corners_landed(hbuf, HS, HCORNER)

    @pl.loop(0, 2)
    def _(i):
        result(i * (rows - HS), 0, HS, HS)
        result(i * (rows - HS), cols - HS, HS, HS)

    deliver(1, 0, HS)
    deliver(2, cols - HS, HS)
    for keep, theirs, ridx in given:
        landed(theirs, ridx)
        keep.wait()
    for there, what in sends:
        if there is None:
            what.wait_send()
        else:
            @pl.when(there)
            def _(what=what):
                what.wait_send()


def solution(mesh):
    nrow, ncol = mesh.shape["row"], mesh.shape["col"]

    def per_device(grad_out, pre_act, weight_one, weight_two):
        batch, rows, cols, chan = grad_out.shape
        strip = rows // 2
        kind = grad_out.dtype
        out = pl.pallas_call(
            functools.partial(kernel, nrow, ncol),
            out_shape=jax.ShapeDtypeStruct((rows, cols, batch, chan), kind),
            in_specs=[pl.BlockSpec(memory_space=pltpu.VMEM), pl.BlockSpec(memory_space=pl.ANY)] + [pl.BlockSpec(memory_space=pltpu.VMEM)] * 2,
            out_specs=pl.BlockSpec(memory_space=pl.ANY),
            scratch_shapes=[
                pltpu.VMEM((2, strip + 2 * GS, cols + 2 * GS, batch, chan), kind),
                pltpu.VMEM((2, strip, cols, batch, chan), kind),
                pltpu.VMEM((2, strip + 2 * HS, cols + 2 * HS, batch, chan), kind),
                pltpu.VMEM((2, strip, cols, batch, chan), kind),
                pltpu.VMEM((strip, GS, batch, chan), kind),
                pltpu.VMEM((2, strip, HS, batch, chan), kind),
                pltpu.VMEM((2, batch, strip, cols, chan), kind),
                pltpu.VMEM((rows, cols, batch, chan), kind),
                pltpu.VMEM((9 * 2 * chan, 2 * chan), kind),
                pltpu.VMEM((9 * 2 * chan, 2 * chan), kind),
                pltpu.SemaphoreType.DMA((32,)),
                pltpu.SemaphoreType.DMA((27,)),
                pltpu.SemaphoreType.DMA((5,)),
            ],
            compiler_params=pltpu.CompilerParams(
                collective_id=0, has_side_effects=True, vmem_limit_bytes=48 * 1024 * 1024),
            cost_estimate=pl.CostEstimate(
                flops=4 * 9 * batch * rows * cols * chan * 2 * chan, bytes_accessed=8 * batch * rows * cols * chan,
                transcendentals=0),
        )(grad_out, pre_act, weight_one, weight_two)
        return jnp.transpose(out, (2, 0, 1, 3))

    placed = (P(None, "row", "col", "filt"), P(None, "row", "col", "filt"), P(), P())
    return jax.shard_map(
        per_device, mesh=mesh, in_specs=placed, out_specs=P(None, "row", "col", "filt"), check_vma=False)
```

```python
import functools

import jax
import jax.numpy as jnp
from jax import lax
from jax.experimental import pallas as pl
from jax.experimental.pallas import tpu as pltpu
from jax.sharding import PartitionSpec as P

MESH = pl.DeviceIdType.MESH
GS = 4
HS = 2


def conv(buf, weight, row, col, rows, cols, spacing):
    batch = buf.shape[3]
    pieces = []
    for p in range(3):
        for q in range(3):
            for half in range(2):
                piece = buf[half, pl.ds(row + spacing * (2 - p), rows), pl.ds(col + spacing * (2 - q), cols)]
                pieces.append(piece.reshape(rows * cols * batch, piece.shape[-1]))
    return jnp.dot(jnp.concatenate(pieces, axis=1), weight[...], preferred_element_type=jnp.float32)


def kernel(nrow, ncol, g_raw, p_in, k1, k2, out, gbuf, pbuf, hbuf, obuf, gvia, hvia, praw, g_in, w1, w2, send, recv, local):
    r, c, f = lax.axis_index("row"), lax.axis_index("col"), lax.axis_index("filt")
    o = 1 - f
    rows = g_in.shape[0] // 2
    cols = g_in.shape[1]
    batch, chan = g_in.shape[2], g_in.shape[3]
    has_left, has_right = c > 0, c < ncol - 1
    has_top, has_bot = r > 0, r < nrow - 1
    first, last = jnp.logical_and(f == 0, r == 0), jnp.logical_and(f == 1, r == nrow - 1)
    has_up, has_down = jnp.logical_not(first), jnp.logical_not(last)
    up = (r - o, c, o)
    down = (r + f, c, o)
    partner = (r, c, o)
    folded = ncol == 4
    across = lax.rem(c + 2, 4)

    @pl.when(first)
    def _():
        gbuf[:, :GS] = jnp.zeros((2, GS) + gbuf.shape[2:], gbuf.dtype)
        hbuf[:, :HS] = jnp.zeros((2, HS) + hbuf.shape[2:], hbuf.dtype)

    @pl.when(last)
    def _():
        gbuf[:, rows + GS:] = jnp.zeros((2, GS) + gbuf.shape[2:], gbuf.dtype)
        hbuf[:, rows + HS:] = jnp.zeros((2, HS) + hbuf.shape[2:], hbuf.dtype)

    @pl.when(jnp.logical_not(has_left))
    def _():
        gbuf[:, :, :GS] = jnp.zeros((2, rows + 2 * GS, GS, batch, chan), gbuf.dtype)
        hbuf[:, :, :HS] = jnp.zeros((2, rows + 2 * HS, HS, batch, chan), hbuf.dtype)

    @pl.when(jnp.logical_not(has_right))
    def _():
        gbuf[:, :, cols + GS:] = jnp.zeros((2, rows + 2 * GS, GS, batch, chan), gbuf.dtype)
        hbuf[:, :, cols + HS:] = jnp.zeros((2, rows + 2 * HS, HS, batch, chan), hbuf.dtype)

    barrier = pltpu.get_barrier_semaphore()
    pl.semaphore_signal(barrier, inc=1, device_id=partner, device_id_type=MESH)
    count = jnp.int32(1)
    for there, rr, cc in ((has_left, r, c - 1), (has_right, r, c + 1), (has_top, r - 1, c), (has_bot, r + 1, c)):
        @pl.when(there)
        def _(rr=rr, cc=cc):
            for ff in range(2):
                pl.semaphore_signal(barrier, inc=1, device_id=(rr, cc, ff), device_id_type=MESH)
        count = count + jnp.where(there, 2, 0)
    if folded:
        pl.semaphore_signal(barrier, inc=1, device_id=(r, across, f), device_id_type=MESH)
        count = count + 1

    @pl.loop(0, 2 * rows, unroll=4)
    def _(y):
        g_in[y] = jnp.swapaxes(g_raw[:, y], 0, 1)

    pl.semaphore_wait(barrier, count)

    def copy(src, dst, sidx, ridx, device):
        return pltpu.make_async_remote_copy(
            src_ref=src, dst_ref=dst, send_sem=send.at[sidx], recv_sem=recv.at[ridx],
            device_id=device, device_id_type=MESH)

    def landed(dst, ridx):
        copy(dst, dst, 0, ridx, partner).wait_recv()

    sends = []

    def start(there, src, dst, ridx, device):
        sidx = len(sends)
        what = copy(src, dst, sidx, ridx, device)
        sends.append((there, what))
        if there is None:
            what.start()
        else:
            @pl.when(there)
            def _():
                what.start()

    grow, gcol = pl.ds(GS, rows), pl.ds(GS, cols)
    hrow, hcol = pl.ds(HS, rows), pl.ds(HS, cols)
    L, R, T, B, MAIN, PRE, CORNER, HL, HR, HT, HB, HCORNER, OUT, VIA, HVIA = (
        0, 2, 4, 6, 8, 9, 10, 14, 15, 16, 17, 18, 22, 23, 24)
    OUTS = (OUT, 25, 26)

    if folded:
        start(c == 1, g_in.at[pl.ds(rows, rows), pl.ds(cols - GS, GS)], gvia, VIA, (r, across, f))
        start(c == 2, g_in.at[pl.ds(rows, rows), pl.ds(0, GS)], gvia, VIA, (r, across, f))
    for ff in range(2):
        to_right, to_left = has_right, has_left
        if folded and ff == 1:
            to_right = jnp.logical_and(has_right, c != 1)
            to_left = jnp.logical_and(has_left, c != 2)
        start(to_right, g_in.at[pl.ds(rows * ff, rows), pl.ds(cols - GS, GS)], gbuf.at[f, grow, pl.ds(0, GS)],
              L + f, (r, c + 1, ff))
        start(to_left, g_in.at[pl.ds(rows * ff, rows), pl.ds(0, GS)], gbuf.at[f, grow, pl.ds(cols + GS, GS)],
              R + f, (r, c - 1, ff))
    span = rows + GS
    start(None, g_in.at[pl.ds((rows - GS) * o, span)], gbuf.at[f, pl.ds(GS * f, span), gcol], MAIN, partner)
    mine = pltpu.make_async_copy(
        g_in.at[pl.ds((rows - GS) * f, span)], gbuf.at[f, pl.ds(GS * o, span), gcol], local.at[0])
    mine.start()
    start(has_bot, g_in.at[pl.ds(2 * rows - GS, GS)], gbuf.at[f, pl.ds(0, GS), gcol], T + f, (r + 1, c, 0))
    start(has_top, g_in.at[pl.ds(0, GS)], gbuf.at[f, pl.ds(rows + GS, GS), gcol], B + f, (r - 1, c, 1))
    start(None, p_in.at[:, pl.ds(rows * o, rows)], praw.at[f], PRE, partner)
    own_pre = pltpu.make_async_copy(p_in.at[:, pl.ds(rows * f, rows)], praw.at[f], local.at[1])
    own_pre.start()

    for src, dst in ((k2, w2), (k1, w1)):
        depth = src.shape[3]
        for p in range(3):
            for q in range(3):
                dst[pl.ds((3 * p + q) * depth, depth)] = src[p, q].T

    if folded:
        @pl.when(jnp.logical_or(c == 0, c == 3))
        def _():
            landed(gvia, VIA)
        start(c == 3, gvia, gbuf.at[f, grow, pl.ds(0, GS)], L + f, (r, c - 1, 1))
        start(c == 0, gvia, gbuf.at[f, grow, pl.ds(cols + GS, GS)], R + f, (r, c + 1, 1))

    landed(gbuf.at[o, pl.ds(GS * o, span), gcol], MAIN)
    mine.wait()
    landed(praw.at[o], PRE)
    own_pre.wait()

    @pl.loop(0, rows, unroll=2)
    def _(y):
        for half in range(2):
            pbuf[half, y] = jnp.swapaxes(praw[half, :, y], 0, 1)

    @pl.when(jnp.logical_and(f == 0, has_top))
    def _():
        for half in range(2):
            landed(gbuf.at[half, pl.ds(0, GS), gcol], T + half)

    @pl.when(jnp.logical_and(f == 1, has_bot))
    def _():
        for half in range(2):
            landed(gbuf.at[half, pl.ds(rows + GS, GS), gcol], B + half)

    def hidden(row, col, nr, nc):
        total = conv(gbuf, w2, row, col, nr, nc, GS)
        for half in range(2):
            keep = pbuf[half, pl.ds(row, nr), pl.ds(col, nc)].reshape(nr * nc * batch, chan).astype(jnp.float32) > 0
            part = jnp.where(keep, total[:, half * chan:(half + 1) * chan], 0.0).astype(hbuf.dtype)
            hbuf[half, pl.ds(row + HS, nr), pl.ds(col + HS, nc)] = part.reshape(nr, nc, batch, chan)

    @pl.loop(0, rows // 4)
    def _(i):
        hidden(i * 4, GS, 4, cols - 2 * GS)

    @pl.when(has_left)
    def _():
        for half in range(2):
            landed(gbuf.at[half, grow, pl.ds(0, GS)], L + half)

    @pl.when(has_right)
    def _():
        for half in range(2):
            landed(gbuf.at[half, grow, pl.ds(cols + GS, GS)], R + half)

    both = pl.ds(0, 2)

    def corners(buf, width, size, base):
        for side, there, col in ((0, has_left, 0), (1, has_right, cols + width)):
            at = pl.ds(col, width)
            start(jnp.logical_and(there, has_up), buf.at[both, pl.ds(width, width), at],
                  buf.at[both, pl.ds(rows + width, width), at], base + side, up)
            start(jnp.logical_and(there, has_down), buf.at[both, pl.ds(rows, width), at],
                  buf.at[both, pl.ds(0, width), at], base + 2 + side, down)

    def corners_landed(buf, width, base):
        for side, there, col in ((0, has_left, 0), (1, has_right, cols + width)):
            at = pl.ds(col, width)

            @pl.when(jnp.logical_and(there, has_down))
            def _(side=side, at=at):
                landed(buf.at[both, pl.ds(rows + width, width), at], base + side)

            @pl.when(jnp.logical_and(there, has_up))
            def _(side=side, at=at):
                landed(buf.at[both, pl.ds(0, width), at], base + 2 + side)

    corners(gbuf, GS, GS, CORNER)

    @pl.loop(1, rows // 4 - 1)
    def _(i):
        hidden(i * 4, 0, 4, GS)
        hidden(i * 4, cols - GS, 4, GS)

    corners_landed(gbuf, GS, CORNER)

    @pl.loop(0, 2)
    def _(i):
        at = i * (rows - 4)
        hidden(at, 0, 4, GS)
        hidden(at, cols - GS, 4, GS)

    to_right, to_left = has_right, has_left
    if folded:
        start(jnp.logical_and(c == 1, f == 1), hbuf.at[both, hrow, pl.ds(cols, HS)], hvia, HVIA, (r, across, f))
        start(jnp.logical_and(c == 2, f == 1), hbuf.at[both, hrow, pl.ds(HS, HS)], hvia, HVIA, (r, across, f))
        to_right = jnp.logical_and(has_right, jnp.logical_or(c != 1, f == 0))
        to_left = jnp.logical_and(has_left, jnp.logical_or(c != 2, f == 0))
    start(to_right, hbuf.at[both, hrow, pl.ds(cols, HS)], hbuf.at[both, hrow, pl.ds(0, HS)], HL, (r, c + 1, f))
    start(to_left, hbuf.at[both, hrow, pl.ds(HS, HS)], hbuf.at[both, hrow, pl.ds(cols + HS, HS)], HR, (r, c - 1, f))
    start(has_up, hbuf.at[both, pl.ds(HS, HS), hcol], hbuf.at[both, pl.ds(rows + HS, HS), hcol], HB, up)
    start(has_down, hbuf.at[both, pl.ds(rows, HS), hcol], hbuf.at[both, pl.ds(0, HS), hcol], HT, down)

    def result(row, col, nr, nc):
        total = conv(hbuf, w1, row, col, nr, nc, HS)
        for half in range(2):
            part = total[:, half * chan:(half + 1) * chan].astype(obuf.dtype)
            obuf[half, pl.ds(row, nr), pl.ds(col, nc)] = part.reshape(nr, nc, batch, chan)

    @pl.loop(0, (rows - 2 * HS) // 4)
    def _(i):
        result(HS + i * 4, HS, 4, cols - 2 * HS)

    if folded:
        @pl.when(jnp.logical_and(jnp.logical_or(c == 0, c == 3), f == 1))
        def _():
            landed(hvia, HVIA)
        start(jnp.logical_and(c == 3, f == 1), hvia, hbuf.at[both, hrow, pl.ds(0, HS)], HL, (r, c - 1, f))
        start(jnp.logical_and(c == 0, f == 1), hvia, hbuf.at[both, hrow, pl.ds(cols + HS, HS)], HR, (r, c + 1, f))

    @pl.when(has_up)
    def _():
        landed(hbuf.at[both, pl.ds(0, HS), hcol], HT)

    @pl.when(has_down)
    def _():
        landed(hbuf.at[both, pl.ds(rows + HS, HS), hcol], HB)

    @pl.loop(0, 2)
    def _(i):
        result(i * (rows - HS), HS, HS, cols - 2 * HS)

    given = []

    def deliver(part, col, nc):
        at = pl.ds(col, nc)
        own = out.at[pl.ds(rows * f, rows), at]
        ridx = OUTS[part]
        start(None, obuf.at[o, pl.ds(0, rows), at], own, ridx, partner)
        keep = pltpu.make_async_copy(obuf.at[f, pl.ds(0, rows), at], own, local.at[2 + part])
        keep.start()
        given.append((keep, out.at[pl.ds(rows * o, rows), at], ridx))

    deliver(0, HS, cols - 2 * HS)

    @pl.when(has_left)
    def _():
        landed(hbuf.at[both, hrow, pl.ds(0, HS)], HL)

    @pl.when(has_right)
    def _():
        landed(hbuf.at[both, hrow, pl.ds(cols + HS, HS)], HR)

    corners(hbuf, HS, HS, HCORNER)

    @pl.loop(0, 2)
    def _(i):
        result(HS, i * (cols - HS), rows - 2 * HS, HS)

    corners_landed(hbuf, HS, HCORNER)

    @pl.loop(0, 2)
    def _(i):
        result(i * (rows - HS), 0, HS, HS)
        result(i * (rows - HS), cols - HS, HS, HS)

    deliver(1, 0, HS)
    deliver(2, cols - HS, HS)
    for keep, theirs, ridx in given:
        landed(theirs, ridx)
        keep.wait()
    for there, what in sends:
        if there is None:
            what.wait_send()
        else:
            @pl.when(there)
            def _(what=what):
                what.wait_send()


def solution(mesh):
    nrow, ncol = mesh.shape["row"], mesh.shape["col"]

    def per_device(grad_out, pre_act, weight_one, weight_two):
        batch, rows, cols, chan = grad_out.shape
        strip = rows // 2
        kind = grad_out.dtype
        out = pl.pallas_call(
            functools.partial(kernel, nrow, ncol),
            out_shape=jax.ShapeDtypeStruct((rows, cols, batch, chan), kind),
            in_specs=[pl.BlockSpec(memory_space=pltpu.VMEM), pl.BlockSpec(memory_space=pl.ANY)] + [pl.BlockSpec(memory_space=pltpu.VMEM)] * 2,
            out_specs=pl.BlockSpec(memory_space=pl.ANY),
            scratch_shapes=[
                pltpu.VMEM((2, strip + 2 * GS, cols + 2 * GS, batch, chan), kind),
                pltpu.VMEM((2, strip, cols, batch, chan), kind),
                pltpu.VMEM((2, strip + 2 * HS, cols + 2 * HS, batch, chan), kind),
                pltpu.VMEM((2, strip, cols, batch, chan), kind),
                pltpu.VMEM((strip, GS, batch, chan), kind),
                pltpu.VMEM((2, strip, HS, batch, chan), kind),
                pltpu.VMEM((2, batch, strip, cols, chan), kind),
                pltpu.VMEM((rows, cols, batch, chan), kind),
                pltpu.VMEM((9 * 2 * chan, 2 * chan), kind),
                pltpu.VMEM((9 * 2 * chan, 2 * chan), kind),
                pltpu.SemaphoreType.DMA((32,)),
                pltpu.SemaphoreType.DMA((27,)),
                pltpu.SemaphoreType.DMA((5,)),
            ],
            compiler_params=pltpu.CompilerParams(
                collective_id=0, has_side_effects=True, vmem_limit_bytes=48 * 1024 * 1024),
            cost_estimate=pl.CostEstimate(
                flops=4 * 9 * batch * rows * cols * chan * 2 * chan, bytes_accessed=8 * batch * rows * cols * chan,
                transcendentals=0),
        )(grad_out, pre_act, weight_one, weight_two)
        return jnp.transpose(out, (2, 0, 1, 3))

    placed = (P(None, "row", "col", "filt"), P(None, "row", "col", "filt"), P(), P())
    return jax.shard_map(
        per_device, mesh=mesh, in_specs=placed, out_specs=P(None, "row", "col", "filt"), check_vma=False)
```
